32 devices in a mesh: pipe: 2 (over x), ctx: 8 (over z, y), tp: 2 (over core).
Axes of the slice: x: 2, y: 2, z: 4, core: 2. Of those that a mesh axis runs over, the one named last changes fastest.
Arguments:
- resid_in: bfloat16 [1024, 4096], P('ctx', 'tp'), may hold values from -6 to 6
- ssm_input: bfloat16 [1024, 8192], P('ctx', 'tp'), may hold values from -6 to 6
- ssm_gate: bfloat16 [1024, 8192], P('ctx', 'tp'), may hold values from -6 to 6
- ssm_in_b: bfloat16 [1024, 512], P('ctx', 'tp'), may hold values from -0.5 to 0.5
- ssm_out_c: bfloat16 [1024, 512], P('ctx', 'tp'), may hold values from -6 to 6
- step_size: float32 [1024, 128], P('ctx', 'tp'), as said below
- decay_rate: float32 [128], P('tp'), may hold values from 0.0001 to 1, as said below
- skip_gain: float32 [128], P('tp'), may hold values from 0.5 to 1.5
- norm_gain: float32 [8192], P('tp'), may hold values from 0.1 to 1.9
- queries: bfloat16 [1024, 8192], P('ctx', 'tp'), may hold values from -6 to 6
- keys: bfloat16 [1024, 512], P('ctx', 'tp'), may hold values from -6 to 6
- values: bfloat16 [1024, 512], P('ctx', 'tp'), may hold values from -6 to 6
- out_weights: bfloat16 [2, 8192, 4096], P('pipe', 'tp', 'ctx'), may hold values from -0.0625 to 0.0625
Outputs:
- sections_out: bfloat16 [2, 1024, 4096], P('pipe', 'ctx', 'tp')
The draws below stay inside these ranges and needn't reach their ends.
Inputs may be any that keep to these rules, and one draw needn't show every extreme that they name: `step_size`: step sizes are positive. `decay_rate`: rates are positive.
All inputs are finite; a program needn't handle non-finite values.
Results may differ from the reference program's by a relative error of at most 0.015.
Values may be sent and summed in bfloat16 or wider, within the bound.
A program may use at most 256 MiB of HBM per device.

```python
import math
import jax
import jax.numpy as jnp
from jax import lax

D = 4096
MHEADS = 128
MHEAD_DIM = 64
STATE = 128
GROUPS = 4
SCAN_BLOCK = 128
QHEADS = 64
KVHEADS = 4
HEAD_DIM = 128
TOKENS = 1024
INNER = 8192
SECTIONS = 2


def forgetting_expression(key):
    parts = jax.random.split(jax.random.fold_in(key, 7), 6)
    cutoff = 5
    quick_route = jax.random.randint(parts[0], (MHEADS,), 0, 10) < cutoff
    spans = jnp.where(quick_route, jax.random.uniform(parts[1], (MHEADS,), minval=30.0, maxval=50.0), TOKENS / jax.random.uniform(parts[1], (MHEADS,), minval=1.0, maxval=1.25))
    baseline = jax.random.uniform(parts[2], (MHEADS,), minval=0.7, maxval=1.4) / jnp.sqrt(spans)
    forgetting_speeds = 1.0 / (spans * baseline)
    rough = jnp.exp(jax.random.uniform(parts[3], (TOKENS, MHEADS), minval=math.log(0.6), maxval=math.log(1.5)))
    increment_widths = baseline[None, :] * rough
    location_indices = jax.random.randint(parts[4], (2, MHEADS), 0, TOKENS)
    all_lines_mask = jnp.arange(TOKENS, dtype=jnp.int32)[:, None]
    element_batch = ((all_lines_mask == location_indices[0][None, :]) | (all_lines_mask == location_indices[1][None, :])) & jnp.logical_not(quick_route)[None, :]
    overall_quantity = jax.random.uniform(parts[5], (MHEADS,), minval=0.22, maxval=0.35)
    increment_widths = jnp.where(element_batch, (overall_quantity / forgetting_speeds)[None, :], increment_widths)
    attenuation_multiplier = 1.0 / (overall_quantity * spans)
    return (forgetting_speeds, increment_widths, element_batch, attenuation_multiplier)


def draw_step_size(key, part):
    return forgetting_expression(key)[1]


def draw_decay_rate(key, part):
    return forgetting_expression(key)[0]


def draw_ssm_input(key, part):
    forgetting_speeds, increment_widths, element_batch, attenuation_multiplier = forgetting_expression(key)
    inner_key = jax.random.fold_in(key, 19)
    drawn = jnp.clip(jax.random.normal(inner_key, (TOKENS, MHEADS, MHEAD_DIM)), -6.0, 6.0)
    multiplier_coefficient = jnp.where(element_batch, attenuation_multiplier[None, :], 1.0)[:, :, None]
    return (drawn * multiplier_coefficient).reshape(TOKENS, MHEADS * MHEAD_DIM).astype(jnp.bfloat16)


def drawn_pair(key):
    parts = jax.random.split(jax.random.fold_in(key, 13), 2)
    query_vals = jnp.clip(jax.random.normal(parts[0], (TOKENS, QHEADS * HEAD_DIM)) * 1.6, -6.0, 6.0)
    key_vals = jnp.clip(jax.random.normal(parts[1], (TOKENS, KVHEADS * HEAD_DIM)) * 1.6, -6.0, 6.0)
    return (query_vals, key_vals)


def draw_queries(key, part):
    return drawn_pair(key)[0].astype(jnp.bfloat16)


def draw_keys(key, part):
    return drawn_pair(key)[1].astype(jnp.bfloat16)


def shard_levels(stream_key, shape, shards, smallest, top_value):
    factor_of, own = 1.0, jax.random.fold_in(stream_key, 6)
    for position, blocks in shards:
        heights = jnp.exp(jax.random.uniform(jax.random.fold_in(own, position), (blocks,), jnp.float32, smallest / len(shards), top_value / len(shards)))
        factor_of = factor_of * jnp.repeat(heights, shape[position] // blocks).reshape([-1 if axis == position else 1 for axis in range(len(shape))])
    return factor_of


def centred(rng, extent, scale, bound, cuts=(), held_as=jnp.bfloat16):
    entries = jax.random.normal(rng, extent, jnp.float32) * scale
    if len(cuts) > 0:
        entries = shard_levels(rng, extent, cuts, -0.22, 0.18) * entries
    return jnp.clip(entries, min=-bound, max=bound).astype(held_as)


def setup_inputs(seed: int = 0) -> dict:
    splits = jax.random.split(jax.random.key(seed), 14)
    resid_in = centred(splits[0], (TOKENS, D), 1.0, 6.0, ((0, 8), (1, 2)))
    ssm_input = draw_ssm_input(jax.random.fold_in(splits[13], 71), 0)
    ssm_gate = centred(splits[2], (TOKENS, INNER), 1.0, 6.0, ((0, 8), (1, 2)))
    ssm_in_b = centred(splits[3], (TOKENS, GROUPS * STATE), STATE ** -0.5, 0.5, ((0, 8), (1, 2)))
    ssm_out_c = centred(splits[4], (TOKENS, GROUPS * STATE), 1.0, 6.0, ((0, 8), (1, 2)))
    step_size = draw_step_size(jax.random.fold_in(splits[13], 71), 0)
    decay_rate = draw_decay_rate(jax.random.fold_in(splits[13], 71), 0)
    skip_gain = jnp.clip(0.5 + 1.0 * jax.random.uniform(splits[7], (MHEADS,), jnp.float32) ** shard_levels(splits[7], (MHEADS,), ((0, 2),), -0.2, 0.2), 0.5, 1.5)
    norm_gain = jnp.clip(1.0 + 0.18 * jax.random.normal(splits[8], (INNER,), jnp.float32), 0.1, 1.9)
    queries = draw_queries(jax.random.fold_in(splits[13], 71), 0)
    keys = draw_keys(jax.random.fold_in(splits[13], 71), 0)
    values = centred(splits[11], (TOKENS, KVHEADS * HEAD_DIM), 1.0, 6.0, ((0, 8), (1, 2)))
    out_weights = centred(splits[12], (SECTIONS, INNER, D), INNER ** -0.5, 0.0625, ((0, 2), (1, 2), (2, 8)))
    return {"resid_in": resid_in, "ssm_input": ssm_input, "ssm_gate": ssm_gate, "ssm_in_b": ssm_in_b, "ssm_out_c": ssm_out_c, "step_size": step_size, "decay_rate": decay_rate, "skip_gain": skip_gain, "norm_gain": norm_gain, "queries": queries, "keys": keys, "values": values, "out_weights": out_weights}


exact_mode = lax.Precision.HIGHEST
norm_eps = 1e-05

def block_scan(state_now, inputs_x, input_b, output_c, step_rows, log_decay):
    width = inputs_x.shape[0]
    groups = inputs_x.shape[1]
    per_group = inputs_x.shape[2]
    running = jnp.cumsum(log_decay, axis=0)
    spread = running[:, None, :] - running[None, :, :]
    causal = jnp.arange(width, dtype=jnp.int32)[:, None] >= jnp.arange(width, dtype=jnp.int32)[None, :]
    decay_mat = jnp.exp(jnp.where(causal[:, :, None], spread, -jnp.inf))
    decay_mat = decay_mat.reshape(width, width, groups, per_group).transpose(2, 3, 0, 1)
    cross_cb = jnp.einsum('tgn,sgn->gts', output_c, input_b, precision=exact_mode)
    step_cols = step_rows.reshape(width, groups, per_group).transpose(1, 2, 0)
    mixing = cross_cb[:, None, :, :] * decay_mat * step_cols[:, :, None, :]
    within = jnp.einsum('gjts,sgjp->tgjp', mixing, inputs_x, precision=exact_mode)
    entry = jnp.exp(running).reshape(width, groups, per_group)
    carried = jnp.einsum('tgn,gjpn->tgjp', output_c, state_now, precision=exact_mode) * entry[:, :, :, None]
    tail_weight = (jnp.exp(running[-1][None, :] - running) * step_rows).reshape(width, groups, per_group)
    leaving = jnp.exp(running[-1]).reshape(groups, per_group)
    state_next = leaving[:, :, None, None] * state_now + jnp.einsum('sgj,sgjp,sgn->gjpn', tail_weight, inputs_x, input_b, precision=exact_mode)
    return (state_next, within + carried)

def gate_norm(values_y, gate_in, gains, groups):
    rows_here = values_y.shape[0]
    gated = values_y * jax.nn.silu(gate_in.astype(jnp.float32))
    grouped = gated.reshape(rows_here, groups, -1)
    meansq = lax.optimization_barrier(jnp.mean(grouped * grouped, axis=-1, keepdims=True))
    scaled = (grouped * lax.rsqrt(meansq + norm_eps)).reshape(rows_here, -1)
    return (scaled * gains[None, :]).astype(jnp.bfloat16)

def mamba_reference(ssm_input, ssm_gate, ssm_in_b, ssm_out_c, step_size, decay_rate, skip_gain, norm_gain):
    total_rows = ssm_input.shape[0]
    per_group = MHEADS // GROUPS
    block_count = total_rows // SCAN_BLOCK
    inputs_x = ssm_input.astype(jnp.float32).reshape(block_count, SCAN_BLOCK, GROUPS, per_group, MHEAD_DIM)
    input_b = ssm_in_b.astype(jnp.float32).reshape(block_count, SCAN_BLOCK, GROUPS, STATE)
    output_c = ssm_out_c.astype(jnp.float32).reshape(block_count, SCAN_BLOCK, GROUPS, STATE)
    step_rows = step_size.reshape(block_count, SCAN_BLOCK, MHEADS)
    log_decay = (-step_size * decay_rate[None, :]).reshape(block_count, SCAN_BLOCK, MHEADS)

    def block_turn(state_now, block_data):
        part_x, part_b, part_c, part_step, part_log = block_data
        return block_scan(state_now, part_x, part_b, part_c, part_step, part_log)
    start_state = jnp.zeros((GROUPS, per_group, MHEAD_DIM, STATE), jnp.float32)
    final_state, pieces = lax.scan(block_turn, start_state, (inputs_x, input_b, output_c, step_rows, log_decay))
    skipped = ssm_input.astype(jnp.float32).reshape(total_rows, MHEADS, MHEAD_DIM) * skip_gain[None, :, None]
    values_y = pieces.reshape(total_rows, MHEADS * MHEAD_DIM) + skipped.reshape(total_rows, MHEADS * MHEAD_DIM)
    return gate_norm(values_y, ssm_gate, norm_gain, GROUPS)

def attention_reference(queries, keys, values):
    total_rows = queries.shape[0]
    per_key = QHEADS // KVHEADS
    span = math.gcd(total_rows, 128)
    score_scale = 1.0 / math.sqrt(HEAD_DIM)
    key_all = keys.astype(jnp.float32).reshape(total_rows, KVHEADS, HEAD_DIM)
    value_all = values.astype(jnp.float32).reshape(total_rows, KVHEADS, HEAD_DIM)
    key_pos = jnp.arange(total_rows, dtype=jnp.int32)

    def query_block(block_index):
        begin = block_index * span
        query_rows = lax.dynamic_slice_in_dim(queries, begin, span, 0).astype(jnp.float32)
        query_rows = query_rows.reshape(span, KVHEADS, per_key, HEAD_DIM)
        scores = jnp.einsum('qgjd,kgd->gjqk', query_rows, key_all) * score_scale
        query_pos = begin + jnp.arange(span, dtype=jnp.int32)
        allowed = key_pos[None, :] <= query_pos[:, None]
        row_top = lax.optimization_barrier(jnp.max(jnp.where(allowed, scores, -jnp.inf), axis=-1, keepdims=True))
        weights_exp = jnp.where(allowed, jnp.exp(scores - row_top), 0.0)
        row_total = lax.optimization_barrier(jnp.sum(weights_exp, axis=-1))
        rounded = lax.optimization_barrier(weights_exp.astype(jnp.bfloat16)).astype(jnp.float32)
        mixed = jnp.einsum('gjqk,kgd->gjqd', rounded, value_all) / row_total[..., None]
        return mixed.transpose(2, 0, 1, 3).reshape(span, QHEADS * HEAD_DIM).astype(jnp.bfloat16)
    blocks_out = lax.map(query_block, jnp.arange(total_rows // span, dtype=jnp.int32))
    return blocks_out.reshape(total_rows, QHEADS * HEAD_DIM)

def reference(resid_in, ssm_input, ssm_gate, ssm_in_b, ssm_out_c, step_size, decay_rate, skip_gain, norm_gain, queries, keys, values, out_weights):
    mamba_mixed = mamba_reference(ssm_input, ssm_gate, ssm_in_b, ssm_out_c, step_size, decay_rate, skip_gain, norm_gain)
    attn_mixed = attention_reference(queries, keys, values)
    section_first = (resid_in.astype(jnp.float32) + jnp.dot(mamba_mixed, out_weights[0], preferred_element_type=jnp.float32)).astype(jnp.bfloat16)
    section_second = (section_first.astype(jnp.float32) + jnp.dot(attn_mixed, out_weights[1], preferred_element_type=jnp.float32)).astype(jnp.bfloat16)
    return jnp.stack([section_first, section_second], axis=0)
```

```python
import math

import jax
import jax.numpy as jnp
from jax import lax
from jax.sharding import PartitionSpec as P

MHEAD_DIM = 64
STATE = 128
HEAD_DIM = 128


exact_mode = lax.Precision.HIGHEST
norm_eps = 1e-05


def from_partner(block, axis, distance):
    count = lax.axis_size(axis)
    route = []
    for low in range(count):
        high = low | 1 << distance
        if high != low and high < count:
            route += [(low, high), (high, low)]
    return lax.ppermute(block, axis, route)


def shifted(x, axis, by):
    peers = lax.axis_size(axis)
    pairs = [(i, i + by) for i in range(peers) if 0 <= i + by < peers]
    return lax.ppermute(x, axis, pairs)


def expand(per_head, width):
    return jnp.repeat(per_head, width, axis=1)


def mamba_local(x, b, c, step, rate, skip):
    rows, heads = step.shape
    log_decay = -step * rate[None, :]
    tri = jnp.arange(rows)[:, None] >= jnp.arange(rows)[None, :]
    running = jnp.dot(tri.astype(jnp.float32), log_decay, precision=exact_mode)
    cross = jnp.einsum("tn,sn->ts", c, b, preferred_element_type=jnp.float32)
    spread = running.T[:, :, None] - running.T[:, None, :]
    decay = jnp.exp(jnp.where(tri[None], spread, -jnp.inf))
    mixing = (cross[None] * decay * step.T[:, None, :]).astype(jnp.bfloat16)
    heads_x = x.reshape(rows, heads, MHEAD_DIM)
    within = jnp.einsum("hts,shp->thp", mixing, heads_x, preferred_element_type=jnp.float32)
    xf = x.astype(jnp.float32)
    within = within.reshape(rows, -1) + xf * jnp.repeat(skip, MHEAD_DIM)[None, :]
    tail = jnp.exp(running[-1:] - running) * step
    weighted = (xf * expand(tail, MHEAD_DIM)).astype(jnp.bfloat16)
    state = jnp.einsum("sp,sn->np", weighted, b, preferred_element_type=jnp.float32)
    return running, within, state


def entering_state(running, state):
    peers, position = lax.axis_size("ctx"), lax.axis_index("ctx")
    last = running[-1]
    logs = lax.all_gather(last, "ctx")
    have, total = state, last
    reach = 1
    while reach < peers:
        pairs = [(i, i + reach) for i in range(peers - reach)]
        got = lax.ppermute(have.astype(jnp.bfloat16), "ctx", pairs).astype(jnp.float32)
        have = have + jnp.exp(jnp.repeat(total, MHEAD_DIM))[None, :] * got
        span = jnp.arange(peers)
        inside = (span <= position) & (span > position - 2 * reach)
        total = jnp.sum(jnp.where(inside[:, None], logs, 0.0), axis=0)
        reach *= 2
    pairs = [(i, i + 1) for i in range(peers - 1)]
    return lax.ppermute(have.astype(jnp.bfloat16), "ctx", pairs)


def mamba_mixer(x, gate, b, c, step, rate, skip, gains):
    running, within, state = mamba_local(x, b, c, step, rate, skip)
    entering = entering_state(running, state)
    carried = jnp.dot(c, entering, preferred_element_type=jnp.float32)
    y = within + carried * expand(jnp.exp(running), MHEAD_DIM)
    gated = y * jax.nn.silu(gate.astype(jnp.float32))
    per_group = gated.reshape(gated.shape[0], b.shape[1] // STATE, -1)
    meansq = jnp.mean(per_group * per_group, axis=-1, keepdims=True)
    scaled = (per_group * lax.rsqrt(meansq + norm_eps)).reshape(gated.shape)
    return (scaled * gains[None, :]).astype(jnp.bfloat16)


def attention(queries, keys, values, ctx_rank):
    rows = queries.shape[0]
    both = lax.all_gather(jnp.concatenate([keys, values], axis=1), "ctx", axis=0, tiled=True)
    k, v = both[:, :HEAD_DIM], both[:, HEAD_DIM:]
    heads = queries.shape[1] // HEAD_DIM
    q = queries.reshape(rows, heads, HEAD_DIM)
    scores = jnp.einsum("qjd,kd->jqk", q, k, preferred_element_type=jnp.float32)
    scores = scores * (1.0 / math.sqrt(HEAD_DIM))
    position = ctx_rank * rows + jnp.arange(rows)
    allowed = jnp.arange(k.shape[0])[None, :] <= position[:, None]
    scores = jnp.where(allowed[None], scores, -jnp.inf)
    weights = jnp.exp(scores - jnp.max(scores, axis=-1, keepdims=True))
    total = jnp.sum(weights, axis=-1)
    mixed = jnp.einsum("jqk,kd->qjd", weights.astype(jnp.bfloat16), v, preferred_element_type=jnp.float32)
    return (mixed / total.T[:, :, None]).reshape(rows, -1).astype(jnp.bfloat16)


def take_half(array, axis_dim, section):
    width = array.shape[axis_dim] // 2
    return lax.dynamic_slice_in_dim(array, section * width, width, axis_dim)


def per_device(
    resid_in,
    ssm_input,
    ssm_gate,
    ssm_in_b,
    ssm_out_c,
    step_size,
    decay_rate,
    skip_gain,
    norm_gain,
    queries,
    keys,
    values,
    out_weights,
):
    section = lax.axis_index("pipe")
    ctx_rank = lax.axis_index("ctx")
    mamba_part = mamba_mixer(
        take_half(ssm_input, 1, section),
        take_half(ssm_gate, 1, section),
        take_half(ssm_in_b, 1, section),
        take_half(ssm_out_c, 1, section),
        take_half(step_size, 1, section),
        take_half(decay_rate, 0, section),
        take_half(skip_gain, 0, section),
        take_half(norm_gain, 0, section),
    )
    attn_part = attention(
        take_half(queries, 1, section),
        take_half(keys, 1, section),
        take_half(values, 1, section),
        ctx_rank,
    )
    outgoing = jnp.where(section == 0, attn_part, mamba_part)
    kept_half = jnp.where(section == 0, mamba_part, attn_part)
    incoming = from_partner(outgoing, "pipe", 0)
    mixed_rows = jnp.where(
        section == 0,
        jnp.concatenate([kept_half, incoming], axis=1),
        jnp.concatenate([incoming, kept_half], axis=1),
    )
    peers = lax.axis_size("ctx")
    rows = mixed_rows.shape[0]
    gathered = lax.all_gather(mixed_rows, "ctx", axis=0, tiled=True)
    partial = jnp.dot(gathered, out_weights[0], preferred_element_type=jnp.float32).astype(jnp.bfloat16)
    pieces = lax.all_to_all(partial.reshape(peers, rows, -1), "ctx", 0, 0)
    whole = pieces.transpose(1, 0, 2).reshape(rows, -1)
    projected = lax.psum_scatter(whole, "tp", scatter_dimension=1, tiled=True).astype(jnp.float32)
    own_section = (resid_in.astype(jnp.float32) + projected).astype(jnp.bfloat16)
    received = shifted(own_section, "pipe", 1)
    second_section = (received.astype(jnp.float32) + projected).astype(jnp.bfloat16)
    return jnp.where(section == 0, own_section, second_section)[None]


def solution(mesh):
    return jax.shard_map(
        per_device,
        mesh=mesh,
        in_specs=(
            P("ctx", "tp"),
            P("ctx", "tp"),
            P("ctx", "tp"),
            P("ctx", "tp"),
            P("ctx", "tp"),
            P("ctx", "tp"),
            P("tp"),
            P("tp"),
            P("tp"),
            P("ctx", "tp"),
            P("ctx", "tp"),
            P("ctx", "tp"),
            P("pipe", "tp", "ctx"),
        ),
        out_specs=P("pipe", "ctx", "tp"),
        check_vma=False,
    )
```

```python
import functools
import math

import jax
import jax.numpy as jnp
from jax import lax
from jax.experimental import pallas as pl
from jax.experimental.pallas import tpu as pltpu
from jax.sharding import PartitionSpec as P

MHEAD_DIM = 64
STATE = 128
HEAD_DIM = 128


MESH = pl.DeviceIdType.MESH
exact_mode = lax.Precision.HIGHEST
norm_eps = 1e-05


def share_kernel(n, kv_ref, log_ref, kv_all, log_all, kv_send, kv_recv, log_send, log_recv):
    pipe, me, tp = (lax.axis_index(a) for a in ("pipe", "ctx", "tp"))
    barrier = pltpu.get_barrier_semaphore()
    for k in range(1, n):
        peer = lax.rem(me + k, n)
        pl.semaphore_signal(barrier, inc=1, device_id=(pipe, peer, tp), device_id_type=MESH)
    kv_all[me] = kv_ref[...]
    log_all[me] = log_ref[...]
    pl.semaphore_wait(barrier, n - 1)

    def copies(k, slot):
        target = (pipe, lax.rem(me + k, n), tp)
        return (
            pltpu.make_async_remote_copy(
                kv_ref, kv_all.at[slot], kv_send.at[k], kv_recv.at[slot],
                device_id=target, device_id_type=MESH,
            ),
            pltpu.make_async_remote_copy(
                log_ref, log_all.at[slot], log_send.at[k], log_recv.at[slot],
                device_id=target, device_id_type=MESH,
            ),
        )

    for k in range(1, n):
        for copy in copies(k, me):
            copy.start()
    for k in range(1, n):
        for copy in copies(k, lax.rem(me + k, n)):
            copy.wait_recv()
        for copy in copies(k, me):
            copy.wait_send()


def share(kv, last, n):
    vmem = pl.BlockSpec(memory_space=pltpu.VMEM)
    logs = jnp.broadcast_to(last[None, :], (8, last.shape[0]))
    logs = jnp.pad(logs, ((0, 0), (0, -last.shape[0] % 128)))
    kv_all, log_all = pl.pallas_call(
        functools.partial(share_kernel, n),
        out_shape=(
            jax.ShapeDtypeStruct((n, *kv.shape), kv.dtype),
            jax.ShapeDtypeStruct((n, *logs.shape), logs.dtype),
        ),
        in_specs=[vmem] * 2,
        out_specs=(vmem, vmem),
        scratch_shapes=[pltpu.SemaphoreType.DMA((n,))] * 4,
        compiler_params=pltpu.CompilerParams(
            collective_id=0, has_side_effects=True, vmem_limit_bytes=32 * 2**20
        ),
        name="share",
    )(kv, logs)
    return kv_all.reshape(-1, kv.shape[1]), log_all[:, 0, : last.shape[0]]


def project_kernel(
    n, kept, outgoing, weights, resid, out,
    rows, staged, parts, first,
    row_recv, up_send, down_send, side_send, pipe_send, part_send, part_recv, first_send, first_recv,
):
    pipe, me, tp = (lax.axis_index(a) for a in ("pipe", "ctx", "tp"))
    line, half_n = n // 2, n // 2
    pos = me // 2
    side = me + 1 - 2 * lax.rem(me, 2)
    owner_tp, own_chunk = me // half_n, lax.rem(me, half_n)
    other = 1 - pipe
    width = weights.shape[1]
    depth = kept.shape[1]

    barrier = pltpu.get_barrier_semaphore()
    here = me * 2 + tp
    for k in range(1, 2 * n):
        there = lax.rem(here + k, 2 * n)
        pl.semaphore_signal(
            barrier, inc=1, device_id=(pipe, there // 2, lax.rem(there, 2)), device_id_type=MESH
        )
    pl.semaphore_signal(barrier, inc=1, device_id=(other, me, tp), device_id_type=MESH)
    rows[me, pipe] = kept[...]
    pl.semaphore_wait(barrier, 2 * n)

    def hop(c, h, sem, ctx):
        return pltpu.make_async_remote_copy(
            rows.at[c, h], rows.at[c, h], sem.at[c, h], row_recv.at[c, h],
            device_id=(pipe, ctx, tp), device_id_type=MESH,
        )

    def cross(h):
        return pltpu.make_async_remote_copy(
            outgoing, rows.at[me, h], pipe_send, row_recv.at[me, h],
            device_id=(other, me, tp), device_id_type=MESH,
        )

    up, down = jnp.minimum(me + 2, n - 1), jnp.maximum(me - 2, 0)
    can_up, can_down = pos + 1 < line, pos > 0

    def part_copy(c):
        return pltpu.make_async_remote_copy(
            staged.at[c], parts.at[own_chunk, tp], part_send.at[c], part_recv.at[own_chunk, tp],
            device_id=(pipe, c, owner_tp), device_id_type=MESH,
        )

    def is_mine(c):
        return (c == me) & (owner_tp == tp)

    cross(pipe).start()

    def forward(s, act):
        @pl.when(s == 0)
        def _():
            for turn in range(2):
                h = pipe if turn == 0 else other
                if turn == 1:
                    act(cross(other), None)

                @pl.when(can_up)
                def _():
                    act(None, hop(me, h, up_send, up))

                @pl.when(can_down)
                def _():
                    act(None, hop(me, h, down_send, down))

                act(None, hop(me, h, side_send, side))

        @pl.when((s > 0) & (s < line))
        def _():
            for turn in range(2):
                h = pipe if turn == 0 else other
                below, above = me - 2 * s, me + 2 * s

                @pl.when(below >= 0)
                def _():
                    act(hop(below, h, up_send, up), None)

                    @pl.when(can_up)
                    def _():
                        act(None, hop(below, h, up_send, up))

                    act(None, hop(below, h, side_send, side))

                @pl.when(above < n)
                def _():
                    act(hop(above, h, down_send, down), None)

                    @pl.when(can_down)
                    def _():
                        act(None, hop(above, h, down_send, down))

                    act(None, hop(above, h, side_send, side))

    def go(arrived, leaving):
        if arrived is not None:
            arrived.wait_recv()
        if leaving is not None:
            leaving.start()

    def drain(arrived, leaving):
        if leaving is not None:
            leaving.wait_send()

    def multiply(c):
        total = jnp.dot(rows[c, 0], weights[:depth], preferred_element_type=jnp.float32)
        total += jnp.dot(rows[c, 1], weights[depth:], preferred_element_type=jnp.float32)
        piece = total.astype(jnp.bfloat16)

        @pl.when(is_mine(c))
        def _():
            parts[own_chunk, tp] = piece

        @pl.when(jnp.logical_not(is_mine(c)))
        def _():
            staged[c] = piece
            part_copy(c).start()

    def turn(s, carry):
        forward(s, go)

        def block(k, carry):
            late = k // 2
            dist = s - late
            centre = me + late * (side - me)
            c = centre + (2 * lax.rem(k, 2) - 1) * 2 * dist
            ok = (dist >= 0) & (dist < line) & (c >= 0) & (c < n)
            ok = ok & ((dist > 0) | (lax.rem(k, 2) == 0))

            @pl.when(ok)
            def _():
                @pl.when(late == 1)
                def _():
                    for h in range(2):
                        hop(c, h, side_send, side).wait_recv()

                multiply(c)

            return carry

        return lax.fori_loop(0, 4, block, carry)

    lax.fori_loop(0, line + 1, turn, 0)

    def first_copy(q):
        return pltpu.make_async_remote_copy(
            first.at[q], first.at[q], first_send.at[q], first_recv.at[q],
            device_id=(other, me, tp), device_id_type=MESH,
        )

    for q in range(half_n):
        source = tp * half_n + q
        for t in range(2):

            @pl.when(jnp.logical_not((source == me) & (tp == t)))
            def _():
                pltpu.make_async_remote_copy(
                    parts.at[q, t], parts.at[q, t], part_send.at[0], part_recv.at[q, t],
                    device_id=(pipe, side, tp), device_id_type=MESH,
                ).wait_recv()

        total = parts[q, 0].astype(jnp.float32) + parts[q, 1].astype(jnp.float32)
        columns = slice(q * width, (q + 1) * width)

        @pl.when(pipe == 0)
        def _():
            done = (resid[:, columns].astype(jnp.float32) + total).astype(jnp.bfloat16)
            first[q] = done
            out[:, columns] = done
            first_copy(q).start()

        @pl.when(pipe == 1)
        def _():
            first_copy(q).wait_recv()
            out[:, columns] = (first[q].astype(jnp.float32) + total).astype(jnp.bfloat16)

    cross(pipe).wait_send()

    def finish(s, carry):
        forward(s, drain)
        return carry

    lax.fori_loop(0, line, finish, 0)

    def sent(c, carry):
        @pl.when(jnp.logical_not(is_mine(c)))
        def _():
            part_copy(c).wait_send()

        return carry

    lax.fori_loop(0, n, sent, 0)

    @pl.when(pipe == 0)
    def _():
        for q in range(half_n):
            first_copy(q).wait_send()


def project(kept, outgoing, weights, resid, n):
    vmem = pl.BlockSpec(memory_space=pltpu.VMEM)
    count, depth = kept.shape
    width = weights.shape[1]
    dma = pltpu.SemaphoreType.DMA
    return pl.pallas_call(
        functools.partial(project_kernel, n),
        out_shape=jax.ShapeDtypeStruct(resid.shape, jnp.bfloat16),
        in_specs=[vmem] * 4,
        out_specs=vmem,
        scratch_shapes=[
            pltpu.VMEM((n, 2, count, depth), jnp.bfloat16),
            pltpu.VMEM((n, count, width), jnp.bfloat16),
            pltpu.VMEM((n // 2, 2, count, width), jnp.bfloat16),
            pltpu.VMEM((n // 2, count, width), jnp.bfloat16),
            dma((n, 2)), dma((n, 2)), dma((n, 2)), dma((n, 2)), dma(()),
            dma((n,)), dma((n // 2, 2)), dma((n // 2,)), dma((n // 2,)),
        ],
        compiler_params=pltpu.CompilerParams(
            collective_id=1, has_side_effects=True, vmem_limit_bytes=56 * 2**20
        ),
        name="project",
    )(kept, outgoing, weights, resid)


def expand(per_head, width):
    return jnp.repeat(per_head, width, axis=1)


def mamba_local(x, b, c, step, rate, skip):
    rows, heads = step.shape
    log_decay = -step * rate[None, :]
    tri = jnp.arange(rows)[:, None] >= jnp.arange(rows)[None, :]
    running = jnp.dot(tri.astype(jnp.float32), log_decay, precision=exact_mode)
    cross = jnp.einsum("tn,sn->ts", c, b, preferred_element_type=jnp.float32)
    spread = running.T[:, :, None] - running.T[:, None, :]
    decay = jnp.exp(jnp.where(tri[None], spread, -jnp.inf))
    mixing = (cross[None] * decay * step.T[:, None, :]).astype(jnp.bfloat16)
    heads_x = x.reshape(rows, heads, MHEAD_DIM)
    within = jnp.einsum("hts,shp->thp", mixing, heads_x, preferred_element_type=jnp.float32)
    xf = x.astype(jnp.float32)
    within = within.reshape(rows, -1) + xf * jnp.repeat(skip, MHEAD_DIM)[None, :]
    tail = jnp.exp(running[-1:] - running) * step
    weighted = (xf * expand(tail, MHEAD_DIM)).astype(jnp.bfloat16)
    state = jnp.einsum("sp,sn->np", weighted, b, preferred_element_type=jnp.float32)
    return running, within, state


def entering_state(running, state, logs):
    peers, position = lax.axis_size("ctx"), lax.axis_index("ctx")
    last = running[-1]
    have, total = state, last
    reach = 1
    while reach < peers:
        pairs = [(i, i + reach) for i in range(peers - reach)]
        got = lax.ppermute(have.astype(jnp.bfloat16), "ctx", pairs).astype(jnp.float32)
        have = have + jnp.exp(jnp.repeat(total, MHEAD_DIM))[None, :] * got
        span = jnp.arange(peers)
        inside = (span <= position) & (span > position - 2 * reach)
        total = jnp.sum(jnp.where(inside[:, None], logs, 0.0), axis=0)
        reach *= 2
    pairs = [(i, i + 1) for i in range(peers - 1)]
    return lax.ppermute(have.astype(jnp.bfloat16), "ctx", pairs)


def mamba_mixer(running, within, entering, gate, b, c, gains):
    carried = jnp.dot(c, entering, preferred_element_type=jnp.float32)
    y = within + carried * expand(jnp.exp(running), MHEAD_DIM)
    gated = y * jax.nn.silu(gate.astype(jnp.float32))
    per_group = gated.reshape(gated.shape[0], b.shape[1] // STATE, -1)
    meansq = jnp.mean(per_group * per_group, axis=-1, keepdims=True)
    scaled = (per_group * lax.rsqrt(meansq + norm_eps)).reshape(gated.shape)
    return (scaled * gains[None, :]).astype(jnp.bfloat16)


def attention(queries, both, ctx_rank):
    rows = queries.shape[0]
    k, v = both[:, :HEAD_DIM], both[:, HEAD_DIM:]
    heads = queries.shape[1] // HEAD_DIM
    q = queries.reshape(rows, heads, HEAD_DIM)
    scores = jnp.einsum("qjd,kd->jqk", q, k, preferred_element_type=jnp.float32)
    scores = scores * (1.0 / math.sqrt(HEAD_DIM))
    position = ctx_rank * rows + jnp.arange(rows)
    allowed = jnp.arange(k.shape[0])[None, :] <= position[:, None]
    scores = jnp.where(allowed[None], scores, -jnp.inf)
    weights = jnp.exp(scores - jnp.max(scores, axis=-1, keepdims=True))
    total = jnp.sum(weights, axis=-1)
    mixed = jnp.einsum("jqk,kd->qjd", weights.astype(jnp.bfloat16), v, preferred_element_type=jnp.float32)
    return (mixed / total.T[:, :, None]).reshape(rows, -1).astype(jnp.bfloat16)


def take_half(array, axis_dim, section):
    width = array.shape[axis_dim] // 2
    return lax.dynamic_slice_in_dim(array, section * width, width, axis_dim)


def per_device(
    resid_in,
    ssm_input,
    ssm_gate,
    ssm_in_b,
    ssm_out_c,
    step_size,
    decay_rate,
    skip_gain,
    norm_gain,
    queries,
    keys,
    values,
    out_weights,
):
    section = lax.axis_index("pipe")
    ctx_rank = lax.axis_index("ctx")
    peers = lax.axis_size("ctx")
    b = take_half(ssm_in_b, 1, section)
    c = take_half(ssm_out_c, 1, section)
    running, within, state = mamba_local(
        take_half(ssm_input, 1, section),
        b,
        c,
        take_half(step_size, 1, section),
        take_half(decay_rate, 0, section),
        take_half(skip_gain, 0, section),
    )
    kv = jnp.concatenate([take_half(keys, 1, section), take_half(values, 1, section)], axis=1)
    both, logs = share(kv, running[-1], peers)
    entering = entering_state(running, state, logs)
    mamba_part = mamba_mixer(
        running, within, entering, take_half(ssm_gate, 1, section), b, c,
        take_half(norm_gain, 0, section),
    )
    attn_part = attention(take_half(queries, 1, section), both, ctx_rank)
    outgoing = jnp.where(section == 0, attn_part, mamba_part)
    kept_half = jnp.where(section == 0, mamba_part, attn_part)
    return project(kept_half, outgoing, out_weights[0], resid_in, peers)[None]


def solution(mesh):
    return jax.shard_map(
        per_device,
        mesh=mesh,
        in_specs=(
            P("ctx", "tp"),
            P("ctx", "tp"),
            P("ctx", "tp"),
            P("ctx", "tp"),
            P("ctx", "tp"),
            P("ctx", "tp"),
            P("tp"),
            P("tp"),
            P("tp"),
            P("ctx", "tp"),
            P("ctx", "tp"),
            P("ctx", "tp"),
            P("pipe", "tp", "ctx"),
        ),
        out_specs=P("pipe", "ctx", "tp"),
        check_vma=False,
    )
```

```python
import functools
import math

import jax
import jax.numpy as jnp
from jax import lax
from jax.experimental import pallas as pl
from jax.experimental.pallas import tpu as pltpu
from jax.sharding import PartitionSpec as P

MHEAD_DIM = 64
STATE = 128
HEAD_DIM = 128


MESH = pl.DeviceIdType.MESH
exact_mode = lax.Precision.HIGHEST
norm_eps = 1e-05


def share_kernel(n, kv_ref, log_ref, kv_all, log_all, kv_send, kv_recv, log_send, log_recv):
    pipe, me, tp = (lax.axis_index(a) for a in ("pipe", "ctx", "tp"))
    barrier = pltpu.get_barrier_semaphore()
    for k in range(1, n):
        peer = lax.rem(me + k, n)
        pl.semaphore_signal(barrier, inc=1, device_id=(pipe, peer, tp), device_id_type=MESH)
    kv_all[me] = kv_ref[...]
    log_all[me] = log_ref[...]
    pl.semaphore_wait(barrier, n - 1)

    def copies(k, slot):
        target = (pipe, lax.rem(me + k, n), tp)
        return (
            pltpu.make_async_remote_copy(
                kv_ref, kv_all.at[slot], kv_send.at[k], kv_recv.at[slot],
                device_id=target, device_id_type=MESH,
            ),
            pltpu.make_async_remote_copy(
                log_ref, log_all.at[slot], log_send.at[k], log_recv.at[slot],
                device_id=target, device_id_type=MESH,
            ),
        )

    for k in range(1, n):
        for copy in copies(k, me):
            copy.start()
    for k in range(1, n):
        for copy in copies(k, lax.rem(me + k, n)):
            copy.wait_recv()
        for copy in copies(k, me):
            copy.wait_send()


def share(kv, last, n):
    vmem = pl.BlockSpec(memory_space=pltpu.VMEM)
    logs = jnp.broadcast_to(last[None, :], (8, last.shape[0]))
    logs = jnp.pad(logs, ((0, 0), (0, -last.shape[0] % 128)))
    kv_all, log_all = pl.pallas_call(
        functools.partial(share_kernel, n),
        out_shape=(
            jax.ShapeDtypeStruct((n, *kv.shape), kv.dtype),
            jax.ShapeDtypeStruct((n, *logs.shape), logs.dtype),
        ),
        in_specs=[vmem] * 2,
        out_specs=(vmem, vmem),
        scratch_shapes=[pltpu.SemaphoreType.DMA((n,))] * 4,
        compiler_params=pltpu.CompilerParams(
            collective_id=0, has_side_effects=True, vmem_limit_bytes=32 * 2**20
        ),
        name="share",
    )(kv, logs)
    return kv_all.reshape(-1, kv.shape[1]), log_all[:, 0, : last.shape[0]]


def project_kernel(
    n, kept, outgoing, w_own, w_side, resid, out,
    rows, held, given, taken, staged, parts, first,
    row_recv, up_send, down_send, pair_send, give_send, give_recv,
    part_send, part_recv, first_send, first_recv,
):
    pipe, me, tp = (lax.axis_index(a) for a in ("pipe", "ctx", "tp"))
    line, half_n = n // 2, n // 2
    pos, member = me // 2, lax.rem(me, 2)
    side = me + 1 - 2 * member
    other, sibling = 1 - pipe, 1 - tp
    target = pos * 2 + tp
    owner_tp, own_chunk = target // half_n, lax.rem(target, half_n)
    width = w_own.shape[1]

    barrier = pltpu.get_barrier_semaphore()
    here = me * 2 + tp
    for k in range(1, 2 * n):
        there = lax.rem(here + k, 2 * n)
        pl.semaphore_signal(
            barrier, inc=1, device_id=(pipe, there // 2, lax.rem(there, 2)), device_id_type=MESH
        )
    for ctx in (me, side):
        pl.semaphore_signal(barrier, inc=1, device_id=(other, ctx, tp), device_id_type=MESH)

    @pl.when(member == pipe)
    def _():
        rows[me] = kept[...]

    pl.semaphore_wait(barrier, 2 * n + 1)

    up, down = jnp.minimum(me + 2, n - 1), jnp.maximum(me - 2, 0)
    can_up, can_down = pos + 1 < line, pos > 0

    def hop(c, sem, ctx):
        return pltpu.make_async_remote_copy(
            rows.at[c], rows.at[c], sem.at[c], row_recv.at[c],
            device_id=(pipe, ctx, tp), device_id_type=MESH,
        )

    def keep_copy():
        return pltpu.make_async_remote_copy(
            kept, rows.at[me], pair_send.at[0], row_recv.at[me],
            device_id=(pipe, side, tp), device_id_type=MESH,
        )

    def cross(ctx):
        return pltpu.make_async_remote_copy(
            outgoing, rows.at[me], pair_send.at[1], row_recv.at[me],
            device_id=(other, ctx, tp), device_id_type=MESH,
        )

    @pl.when(member == pipe)
    def _():
        cross(me).start()

    @pl.when(member != pipe)
    def _():
        keep_copy().start()
        cross(side).start()

    def forward(s, start):
        for which in range(2):
            base = me if which == 0 else side
            for way in range(2):
                c = base - 2 * s if way == 0 else base + 2 * s
                ok = (c >= 0) & (c < n)
                if way == 1:
                    ok = ok & (s > 0)

                @pl.when(ok)
                def _():
                    if start:
                        if which == 0:

                            @pl.when((s > 0) | (member != pipe))
                            def _():
                                hop(c, up_send, up).wait_recv()
                        else:
                            hop(c, up_send, up).wait_recv()

                    @pl.when(can_up & ((s == 0) | (way == 0)))
                    def _():
                        copy = hop(c, up_send, up)
                        copy.start() if start else copy.wait_send()

                    @pl.when(can_down & ((s == 0) | (way == 1)))
                    def _():
                        copy = hop(c, down_send, down)
                        copy.start() if start else copy.wait_send()

    def give_copy(c):
        return pltpu.make_async_remote_copy(
            given.at[c], taken.at[c], give_send.at[c], give_recv.at[c],
            device_id=(pipe, me, sibling), device_id_type=MESH,
        )

    def part_copy(c):
        return pltpu.make_async_remote_copy(
            staged.at[c], parts.at[own_chunk, member],
            part_send.at[c], part_recv.at[own_chunk, member],
            device_id=(pipe, c, owner_tp), device_id_type=MESH,
        )

    def is_mine(c):
        return (c == me) & (owner_tp == tp)

    def multiply(c):
        mine = jnp.dot(rows[c], w_own[...], preferred_element_type=jnp.float32)
        theirs = jnp.dot(rows[c], w_side[...], preferred_element_type=jnp.float32)
        straight = member == tp
        held[c] = jnp.where(straight, mine, theirs)
        given[c] = jnp.where(straight, theirs, mine).astype(jnp.bfloat16)
        give_copy(c).start()

    def pass_on(c):
        give_copy(c).wait_recv()
        piece = (held[c] + taken[c].astype(jnp.float32)).astype(jnp.bfloat16)

        @pl.when(is_mine(c))
        def _():
            parts[own_chunk, member] = piece

        @pl.when(jnp.logical_not(is_mine(c)))
        def _():
            staged[c] = piece
            part_copy(c).start()

    def turn(s, carry):
        forward(s, True)

        def each(act):
            def block(k, carry):
                base = me + (k // 2) * (side - me)
                c = base + (2 * lax.rem(k, 2) - 1) * 2 * s

                @pl.when((c >= 0) & (c < n) & ((s > 0) | (lax.rem(k, 2) == 0)))
                def _():
                    act(c)

                return carry

            return block

        lax.fori_loop(0, 4, each(multiply), 0)
        lax.fori_loop(0, 4, each(pass_on), 0)
        return carry

    lax.fori_loop(0, line, turn, 0)

    def first_copy(q):
        return pltpu.make_async_remote_copy(
            first.at[q], first.at[q], first_send.at[q], first_recv.at[q],
            device_id=(other, me, tp), device_id_type=MESH,
        )

    for q in range(half_n):
        source = tp * half_n + q
        for m in range(2):
            from_ctx = source // 2 * 2 + m

            @pl.when(jnp.logical_not((from_ctx == me) & (lax.rem(source, 2) == tp)))
            def _():
                pltpu.make_async_remote_copy(
                    parts.at[q, m], parts.at[q, m], part_send.at[0], part_recv.at[q, m],
                    device_id=(pipe, side, tp), device_id_type=MESH,
                ).wait_recv()

        total = parts[q, 0].astype(jnp.float32) + parts[q, 1].astype(jnp.float32)
        columns = slice(q * width, (q + 1) * width)

        @pl.when(pipe == 0)
        def _():
            done = (resid[:, columns].astype(jnp.float32) + total).astype(jnp.bfloat16)
            first[q] = done
            out[:, columns] = done
            first_copy(q).start()

        @pl.when(pipe == 1)
        def _():
            first_copy(q).wait_recv()
            out[:, columns] = (first[q].astype(jnp.float32) + total).astype(jnp.bfloat16)

    @pl.when(member == pipe)
    def _():
        cross(me).wait_send()

    @pl.when(member != pipe)
    def _():
        keep_copy().wait_send()
        cross(side).wait_send()

    def finish(s, carry):
        forward(s, False)
        return carry

    lax.fori_loop(0, line, finish, 0)

    def sent(c, carry):
        give_copy(c).wait_send()

        @pl.when(jnp.logical_not(is_mine(c)))
        def _():
            part_copy(c).wait_send()

        return carry

    lax.fori_loop(0, n, sent, 0)

    @pl.when(pipe == 0)
    def _():
        for q in range(half_n):
            first_copy(q).wait_send()


def project(kept, outgoing, w_own, w_side, resid, n):
    vmem = pl.BlockSpec(memory_space=pltpu.VMEM)
    count, depth = kept.shape
    width = w_own.shape[1]
    dma = pltpu.SemaphoreType.DMA
    block = (count, width)
    return pl.pallas_call(
        functools.partial(project_kernel, n),
        out_shape=jax.ShapeDtypeStruct(resid.shape, jnp.bfloat16),
        in_specs=[vmem] * 5,
        out_specs=vmem,
        scratch_shapes=[
            pltpu.VMEM((n, count, depth), jnp.bfloat16),
            pltpu.VMEM((n, *block), jnp.float32),
            pltpu.VMEM((n, *block), jnp.bfloat16),
            pltpu.VMEM((n, *block), jnp.bfloat16),
            pltpu.VMEM((n, *block), jnp.bfloat16),
            pltpu.VMEM((n // 2, 2, *block), jnp.bfloat16),
            pltpu.VMEM((n // 2, *block), jnp.bfloat16),
            dma((n,)), dma((n,)), dma((n,)), dma((2,)), dma((n,)), dma((n,)),
            dma((n,)), dma((n // 2, 2)), dma((n // 2,)), dma((n // 2,)),
        ],
        compiler_params=pltpu.CompilerParams(
            collective_id=1, has_side_effects=True, vmem_limit_bytes=56 * 2**20
        ),
        name="project",
    )(kept, outgoing, w_own, w_side, resid)


def expand(per_head, width):
    return jnp.repeat(per_head, width, axis=1)


def mamba_local(x, b, c, step, rate, skip):
    rows, heads = step.shape
    log_decay = -step * rate[None, :]
    tri = jnp.arange(rows)[:, None] >= jnp.arange(rows)[None, :]
    running = jnp.dot(tri.astype(jnp.float32), log_decay, precision=exact_mode)
    cross = jnp.einsum("tn,sn->ts", c, b, preferred_element_type=jnp.float32)
    spread = running.T[:, :, None] - running.T[:, None, :]
    decay = jnp.exp(jnp.where(tri[None], spread, -jnp.inf))
    mixing = (cross[None] * decay * step.T[:, None, :]).astype(jnp.bfloat16)
    heads_x = x.reshape(rows, heads, MHEAD_DIM)
    within = jnp.einsum("hts,shp->thp", mixing, heads_x, preferred_element_type=jnp.float32)
    xf = x.astype(jnp.float32)
    within = within.reshape(rows, -1) + xf * jnp.repeat(skip, MHEAD_DIM)[None, :]
    tail = jnp.exp(running[-1:] - running) * step
    weighted = (xf * expand(tail, MHEAD_DIM)).astype(jnp.bfloat16)
    state = jnp.einsum("sp,sn->np", weighted, b, preferred_element_type=jnp.float32)
    return running, within, state


def entering_state(running, state, logs):
    peers, position = lax.axis_size("ctx"), lax.axis_index("ctx")
    span = jnp.arange(peers)
    own = jnp.exp(jnp.repeat(running[-1], MHEAD_DIM))[None, :]
    before = jnp.zeros_like(state)
    reach = 1
    while reach < peers:
        pairs = [(i, i + reach) for i in range(peers - reach)]
        sent = (state + own * before).astype(jnp.bfloat16)
        got = lax.ppermute(sent, "ctx", pairs).astype(jnp.float32)
        inside = (span < position) & (span > position - reach)
        through = jnp.sum(jnp.where(inside[:, None], logs, 0.0), axis=0)
        before = before + jnp.exp(jnp.repeat(through, MHEAD_DIM))[None, :] * got
        reach *= 2
    return before.astype(jnp.bfloat16)


def mamba_mixer(running, within, entering, gate, b, c, gains):
    carried = jnp.dot(c, entering, preferred_element_type=jnp.float32)
    y = within + carried * expand(jnp.exp(running), MHEAD_DIM)
    gated = y * jax.nn.silu(gate.astype(jnp.float32))
    per_group = gated.reshape(gated.shape[0], b.shape[1] // STATE, -1)
    meansq = jnp.mean(per_group * per_group, axis=-1, keepdims=True)
    scaled = (per_group * lax.rsqrt(meansq + norm_eps)).reshape(gated.shape)
    return (scaled * gains[None, :]).astype(jnp.bfloat16)


def attention(queries, both, ctx_rank):
    rows = queries.shape[0]
    k, v = both[:, :HEAD_DIM], both[:, HEAD_DIM:]
    heads = queries.shape[1] // HEAD_DIM
    q = queries.reshape(rows, heads, HEAD_DIM)
    scores = jnp.einsum("qjd,kd->jqk", q, k, preferred_element_type=jnp.float32)
    scores = scores * (1.0 / math.sqrt(HEAD_DIM))
    position = ctx_rank * rows + jnp.arange(rows)
    allowed = jnp.arange(k.shape[0])[None, :] <= position[:, None]
    scores = jnp.where(allowed[None], scores, -jnp.inf)
    weights = jnp.exp(scores - jnp.max(scores, axis=-1, keepdims=True))
    total = jnp.sum(weights, axis=-1)
    mixed = jnp.einsum("jqk,kd->qjd", weights.astype(jnp.bfloat16), v, preferred_element_type=jnp.float32)
    return (mixed / total.T[:, :, None]).reshape(rows, -1).astype(jnp.bfloat16)


def take_half(array, axis_dim, section):
    width = array.shape[axis_dim] // 2
    return lax.dynamic_slice_in_dim(array, section * width, width, axis_dim)


def per_device(
    resid_in,
    ssm_input,
    ssm_gate,
    ssm_in_b,
    ssm_out_c,
    step_size,
    decay_rate,
    skip_gain,
    norm_gain,
    queries,
    keys,
    values,
    out_weights,
):
    section = lax.axis_index("pipe")
    ctx_rank = lax.axis_index("ctx")
    peers = lax.axis_size("ctx")
    member = lax.rem(ctx_rank, 2)
    w_own = take_half(out_weights[0], 0, member)
    w_side = lax.ppermute(
        take_half(out_weights[0], 0, 1 - member), "ctx", [(i, i ^ 1) for i in range(peers)]
    )
    b = take_half(ssm_in_b, 1, section)
    c = take_half(ssm_out_c, 1, section)
    running, within, state = mamba_local(
        take_half(ssm_input, 1, section),
        b,
        c,
        take_half(step_size, 1, section),
        take_half(decay_rate, 0, section),
        take_half(skip_gain, 0, section),
    )
    kv = jnp.concatenate([take_half(keys, 1, section), take_half(values, 1, section)], axis=1)
    both, logs = share(kv, running[-1], peers)
    entering = entering_state(running, state, logs)
    mamba_part = mamba_mixer(
        running, within, entering, take_half(ssm_gate, 1, section), b, c,
        take_half(norm_gain, 0, section),
    )
    attn_part = attention(take_half(queries, 1, section), both, ctx_rank)
    outgoing = jnp.where(section == 0, attn_part, mamba_part)
    kept_half = jnp.where(section == 0, mamba_part, attn_part)
    return project(kept_half, outgoing, w_own, w_side, resid_in, peers)[None]


def solution(mesh):
    return jax.shard_map(
        per_device,
        mesh=mesh,
        in_specs=(
            P("ctx", "tp"),
            P("ctx", "tp"),
            P("ctx", "tp"),
            P("ctx", "tp"),
            P("ctx", "tp"),
            P("ctx", "tp"),
            P("tp"),
            P("tp"),
            P("tp"),
            P("ctx", "tp"),
            P("ctx", "tp"),
            P("ctx", "tp"),
            P("pipe", "tp", "ctx"),
        ),
        out_specs=P("pipe", "ctx", "tp"),
        check_vma=False,
    )
```

```python
import functools
import math

import jax
import jax.numpy as jnp
from jax import lax
from jax.experimental import pallas as pl
from jax.experimental.pallas import tpu as pltpu
from jax.sharding import PartitionSpec as P

MHEAD_DIM = 64
STATE = 128
HEAD_DIM = 128


MESH = pl.DeviceIdType.MESH
exact_mode = lax.Precision.HIGHEST
norm_eps = 1e-05


def share_kernel(n, kv_ref, log_ref, kv_all, log_all, kv_send, kv_recv, log_send, log_recv):
    pipe, me, tp = (lax.axis_index(a) for a in ("pipe", "ctx", "tp"))
    barrier = pltpu.get_barrier_semaphore()
    for k in range(1, n):
        peer = lax.rem(me + k, n)
        pl.semaphore_signal(barrier, inc=1, device_id=(pipe, peer, tp), device_id_type=MESH)
    kv_all[me] = kv_ref[...]
    log_all[me] = log_ref[...]
    pl.semaphore_wait(barrier, n - 1)

    def copies(k, slot):
        target = (pipe, lax.rem(me + k, n), tp)
        return (
            pltpu.make_async_remote_copy(
                kv_ref, kv_all.at[slot], kv_send.at[k], kv_recv.at[slot],
                device_id=target, device_id_type=MESH,
            ),
            pltpu.make_async_remote_copy(
                log_ref, log_all.at[slot], log_send.at[k], log_recv.at[slot],
                device_id=target, device_id_type=MESH,
            ),
        )

    for k in range(1, n):
        for copy in copies(k, me):
            copy.start()
    for k in range(1, n):
        for copy in copies(k, lax.rem(me + k, n)):
            copy.wait_recv()
        for copy in copies(k, me):
            copy.wait_send()


def share(kv, last, n):
    vmem = pl.BlockSpec(memory_space=pltpu.VMEM)
    logs = jnp.broadcast_to(last[None, :], (8, last.shape[0]))
    logs = jnp.pad(logs, ((0, 0), (0, -last.shape[0] % 128)))
    kv_all, log_all = pl.pallas_call(
        functools.partial(share_kernel, n),
        out_shape=(
            jax.ShapeDtypeStruct((n, *kv.shape), kv.dtype),
            jax.ShapeDtypeStruct((n, *logs.shape), logs.dtype),
        ),
        in_specs=[vmem] * 2,
        out_specs=(vmem, vmem),
        scratch_shapes=[pltpu.SemaphoreType.DMA((n,))] * 4,
        compiler_params=pltpu.CompilerParams(
            collective_id=0, has_side_effects=True, vmem_limit_bytes=32 * 2**20
        ),
        name="share",
    )(kv, logs)
    return kv_all.reshape(-1, kv.shape[1]), log_all[:, 0, : last.shape[0]]


def project_kernel(
    n, kept, outgoing, weights, resid, out,
    rows, staged, parts, first,
    row_recv, up_send, down_send, side_send, pipe_send, part_send, part_recv, first_send, first_recv,
):
    pipe, me, tp = (lax.axis_index(a) for a in ("pipe", "ctx", "tp"))
    line, half_n = n // 2, n // 2
    pos = me // 2
    side = me + 1 - 2 * lax.rem(me, 2)
    owner_tp, own_chunk = me // half_n, lax.rem(me, half_n)
    other = 1 - pipe
    width = weights.shape[1]
    depth = kept.shape[1]

    barrier = pltpu.get_barrier_semaphore()
    here = me * 2 + tp
    for k in range(1, 2 * n):
        there = lax.rem(here + k, 2 * n)
        pl.semaphore_signal(
            barrier, inc=1, device_id=(pipe, there // 2, lax.rem(there, 2)), device_id_type=MESH
        )
    pl.semaphore_signal(barrier, inc=1, device_id=(other, me, tp), device_id_type=MESH)
    rows[me, pipe] = kept[...]
    pl.semaphore_wait(barrier, 2 * n)

    def hop(c, h, sem, ctx):
        return pltpu.make_async_remote_copy(
            rows.at[c, h], rows.at[c, h], sem.at[c, h], row_recv.at[c, h],
            device_id=(pipe, ctx, tp), device_id_type=MESH,
        )

    def cross(h):
        return pltpu.make_async_remote_copy(
            outgoing, rows.at[me, h], pipe_send, row_recv.at[me, h],
            device_id=(other, me, tp), device_id_type=MESH,
        )

    up, down = jnp.minimum(me + 2, n - 1), jnp.maximum(me - 2, 0)
    can_up, can_down = pos + 1 < line, pos > 0

    def part_copy(c):
        return pltpu.make_async_remote_copy(
            staged.at[c], parts.at[own_chunk, tp], part_send.at[c], part_recv.at[own_chunk, tp],
            device_id=(pipe, c, owner_tp), device_id_type=MESH,
        )

    def is_mine(c):
        return (c == me) & (owner_tp == tp)

    cross(pipe).start()

    def forward(s, act):
        @pl.when(s == 0)
        def _():
            for turn in range(2):
                h = pipe if turn == 0 else other
                if turn == 1:
                    act(cross(other), None)

                @pl.when(can_up)
                def _():
                    act(None, hop(me, h, up_send, up))

                @pl.when(can_down)
                def _():
                    act(None, hop(me, h, down_send, down))

                act(None, hop(me, h, side_send, side))

        @pl.when((s > 0) & (s < line))
        def _():
            for turn in range(2):
                h = pipe if turn == 0 else other
                below, above = me - 2 * s, me + 2 * s

                @pl.when(below >= 0)
                def _():
                    act(hop(below, h, up_send, up), None)

                    @pl.when(can_up)
                    def _():
                        act(None, hop(below, h, up_send, up))

                    act(None, hop(below, h, side_send, side))

                @pl.when(above < n)
                def _():
                    act(hop(above, h, down_send, down), None)

                    @pl.when(can_down)
                    def _():
                        act(None, hop(above, h, down_send, down))

                    act(None, hop(above, h, side_send, side))

    def go(arrived, leaving):
        if arrived is not None:
            arrived.wait_recv()
        if leaving is not None:
            leaving.start()

    def drain(arrived, leaving):
        if leaving is not None:
            leaving.wait_send()

    def multiply(c):
        total = jnp.dot(rows[c, 0], weights[:depth], preferred_element_type=jnp.float32)
        total += jnp.dot(rows[c, 1], weights[depth:], preferred_element_type=jnp.float32)
        piece = total.astype(jnp.bfloat16)

        @pl.when(is_mine(c))
        def _():
            parts[own_chunk, tp] = piece

        @pl.when(jnp.logical_not(is_mine(c)))
        def _():
            staged[c] = piece
            part_copy(c).start()

    def turn(s, carry):
        forward(s, go)

        def block(k, carry):
            late = k // 2
            dist = s - late
            centre = me + late * (side - me)
            c = centre + (2 * lax.rem(k, 2) - 1) * 2 * dist
            ok = (dist >= 0) & (dist < line) & (c >= 0) & (c < n)
            ok = ok & ((dist > 0) | (lax.rem(k, 2) == 0))

            @pl.when(ok)
            def _():
                @pl.when(late == 1)
                def _():
                    for h in range(2):
                        hop(c, h, side_send, side).wait_recv()

                multiply(c)

            return carry

        return lax.fori_loop(0, 4, block, carry)

    lax.fori_loop(0, line + 1, turn, 0)

    def first_copy(q):
        return pltpu.make_async_remote_copy(
            first.at[q], first.at[q], first_send.at[q], first_recv.at[q],
            device_id=(other, me, tp), device_id_type=MESH,
        )

    for q in range(half_n):
        source = tp * half_n + q
        for t in range(2):

            @pl.when(jnp.logical_not((source == me) & (tp == t)))
            def _():
                pltpu.make_async_remote_copy(
                    parts.at[q, t], parts.at[q, t], part_send.at[0], part_recv.at[q, t],
                    device_id=(pipe, side, tp), device_id_type=MESH,
                ).wait_recv()

        total = parts[q, 0].astype(jnp.float32) + parts[q, 1].astype(jnp.float32)
        columns = slice(q * width, (q + 1) * width)

        @pl.when(pipe == 0)
        def _():
            done = (resid[:, columns].astype(jnp.float32) + total).astype(jnp.bfloat16)
            first[q] = done
            out[:, columns] = done
            first_copy(q).start()

        @pl.when(pipe == 1)
        def _():
            first_copy(q).wait_recv()
            out[:, columns] = (first[q].astype(jnp.float32) + total).astype(jnp.bfloat16)

    cross(pipe).wait_send()

    def finish(s, carry):
        forward(s, drain)
        return carry

    lax.fori_loop(0, line, finish, 0)

    def sent(c, carry):
        @pl.when(jnp.logical_not(is_mine(c)))
        def _():
            part_copy(c).wait_send()

        return carry

    lax.fori_loop(0, n, sent, 0)

    @pl.when(pipe == 0)
    def _():
        for q in range(half_n):
            first_copy(q).wait_send()


def project(kept, outgoing, weights, resid, n):
    vmem = pl.BlockSpec(memory_space=pltpu.VMEM)
    count, depth = kept.shape
    width = weights.shape[1]
    dma = pltpu.SemaphoreType.DMA
    return pl.pallas_call(
        functools.partial(project_kernel, n),
        out_shape=jax.ShapeDtypeStruct(resid.shape, jnp.bfloat16),
        in_specs=[vmem] * 4,
        out_specs=vmem,
        scratch_shapes=[
            pltpu.VMEM((n, 2, count, depth), jnp.bfloat16),
            pltpu.VMEM((n, count, width), jnp.bfloat16),
            pltpu.VMEM((n // 2, 2, count, width), jnp.bfloat16),
            pltpu.VMEM((n // 2, count, width), jnp.bfloat16),
            dma((n, 2)), dma((n, 2)), dma((n, 2)), dma((n, 2)), dma(()),
            dma((n,)), dma((n // 2, 2)), dma((n // 2,)), dma((n // 2,)),
        ],
        compiler_params=pltpu.CompilerParams(
            collective_id=1, has_side_effects=True, vmem_limit_bytes=56 * 2**20
        ),
        name="project",
    )(kept, outgoing, weights, resid)


def expand(per_head, width):
    return jnp.repeat(per_head, width, axis=1)


def mamba_local(x, b, c, step, rate, skip):
    rows, heads = step.shape
    log_decay = -step * rate[None, :]
    tri = jnp.arange(rows)[:, None] >= jnp.arange(rows)[None, :]
    running = jnp.dot(tri.astype(jnp.float32), log_decay, precision=exact_mode)
    cross = jnp.einsum("tn,sn->ts", c, b, preferred_element_type=jnp.float32)
    spread = running.T[:, :, None] - running.T[:, None, :]
    decay = jnp.exp(jnp.where(tri[None], spread, -jnp.inf))
    mixing = (cross[None] * decay * step.T[:, None, :]).astype(jnp.bfloat16)
    heads_x = x.reshape(rows, heads, MHEAD_DIM)
    within = jnp.einsum("hts,shp->thp", mixing, heads_x, preferred_element_type=jnp.float32)
    xf = x.astype(jnp.float32)
    within = within.reshape(rows, -1) + xf * jnp.repeat(skip, MHEAD_DIM)[None, :]
    tail = jnp.exp(running[-1:] - running) * step
    weighted = (xf * expand(tail, MHEAD_DIM)).astype(jnp.bfloat16)
    state = jnp.einsum("sp,sn->np", weighted, b, preferred_element_type=jnp.float32)
    return running, within, state


def entering_state(running, state, logs):
    peers, position = lax.axis_size("ctx"), lax.axis_index("ctx")
    span = jnp.arange(peers)
    own = jnp.exp(jnp.repeat(running[-1], MHEAD_DIM))[None, :]
    before = jnp.zeros_like(state)
    reach = 1
    while reach < peers:
        pairs = [(i, i + reach) for i in range(peers - reach)]
        sent = (state + own * before).astype(jnp.bfloat16)
        got = lax.ppermute(sent, "ctx", pairs).astype(jnp.float32)
        inside = (span < position) & (span > position - reach)
        through = jnp.sum(jnp.where(inside[:, None], logs, 0.0), axis=0)
        before = before + jnp.exp(jnp.repeat(through, MHEAD_DIM))[None, :] * got
        reach *= 2
    return before.astype(jnp.bfloat16)


def mamba_mixer(running, within, entering, gate, b, c, gains):
    carried = jnp.dot(c, entering, preferred_element_type=jnp.float32)
    y = within + carried * expand(jnp.exp(running), MHEAD_DIM)
    gated = y * jax.nn.silu(gate.astype(jnp.float32))
    per_group = gated.reshape(gated.shape[0], b.shape[1] // STATE, -1)
    meansq = jnp.mean(per_group * per_group, axis=-1, keepdims=True)
    scaled = (per_group * lax.rsqrt(meansq + norm_eps)).reshape(gated.shape)
    return (scaled * gains[None, :]).astype(jnp.bfloat16)


def attention(queries, both, ctx_rank):
    rows = queries.shape[0]
    k, v = both[:, :HEAD_DIM], both[:, HEAD_DIM:]
    heads = queries.shape[1] // HEAD_DIM
    q = queries.reshape(rows, heads, HEAD_DIM)
    scores = jnp.einsum("qjd,kd->jqk", q, k, preferred_element_type=jnp.float32)
    scores = scores * (1.0 / math.sqrt(HEAD_DIM))
    position = ctx_rank * rows + jnp.arange(rows)
    allowed = jnp.arange(k.shape[0])[None, :] <= position[:, None]
    scores = jnp.where(allowed[None], scores, -jnp.inf)
    weights = jnp.exp(scores - jnp.max(scores, axis=-1, keepdims=True))
    total = jnp.sum(weights, axis=-1)
    mixed = jnp.einsum("jqk,kd->qjd", weights.astype(jnp.bfloat16), v, preferred_element_type=jnp.float32)
    return (mixed / total.T[:, :, None]).reshape(rows, -1).astype(jnp.bfloat16)


def take_half(array, axis_dim, section):
    width = array.shape[axis_dim] // 2
    return lax.dynamic_slice_in_dim(array, section * width, width, axis_dim)


def per_device(
    resid_in,
    ssm_input,
    ssm_gate,
    ssm_in_b,
    ssm_out_c,
    step_size,
    decay_rate,
    skip_gain,
    norm_gain,
    queries,
    keys,
    values,
    out_weights,
):
    section = lax.axis_index("pipe")
    ctx_rank = lax.axis_index("ctx")
    peers = lax.axis_size("ctx")
    b = take_half(ssm_in_b, 1, section)
    c = take_half(ssm_out_c, 1, section)
    running, within, state = mamba_local(
        take_half(ssm_input, 1, section),
        b,
        c,
        take_half(step_size, 1, section),
        take_half(decay_rate, 0, section),
        take_half(skip_gain, 0, section),
    )
    kv = jnp.concatenate([take_half(keys, 1, section), take_half(values, 1, section)], axis=1)
    both, logs = share(kv, running[-1], peers)
    entering = entering_state(running, state, logs)
    mamba_part = mamba_mixer(
        running, within, entering, take_half(ssm_gate, 1, section), b, c,
        take_half(norm_gain, 0, section),
    )
    attn_part = attention(take_half(queries, 1, section), both, ctx_rank)
    outgoing = jnp.where(section == 0, attn_part, mamba_part)
    kept_half = jnp.where(section == 0, mamba_part, attn_part)
    return project(kept_half, outgoing, out_weights[0], resid_in, peers)[None]


def solution(mesh):
    return jax.shard_map(
        per_device,
        mesh=mesh,
        in_specs=(
            P("ctx", "tp"),
            P("ctx", "tp"),
            P("ctx", "tp"),
            P("ctx", "tp"),
            P("ctx", "tp"),
            P("ctx", "tp"),
            P("tp"),
            P("tp"),
            P("tp"),
            P("ctx", "tp"),
            P("ctx", "tp"),
            P("ctx", "tp"),
            P("pipe", "tp", "ctx"),
        ),
        out_specs=P("pipe", "ctx", "tp"),
        check_vma=False,
    )
```

```python
import functools
import math

import jax
import jax.numpy as jnp
from jax import lax
from jax.experimental import pallas as pl
from jax.experimental.pallas import tpu as pltpu
from jax.sharding import PartitionSpec as P

MHEAD_DIM = 64
STATE = 128
HEAD_DIM = 128


MESH = pl.DeviceIdType.MESH
exact_mode = lax.Precision.HIGHEST
norm_eps = 1e-05


def share_kernel(n, kv_ref, log_ref, kv_all, log_all, kv_send, kv_recv, log_send, log_recv):
    pipe, me, tp = (lax.axis_index(a) for a in ("pipe", "ctx", "tp"))
    barrier = pltpu.get_barrier_semaphore()
    for k in range(1, n):
        peer = lax.rem(me + k, n)
        pl.semaphore_signal(barrier, inc=1, device_id=(pipe, peer, tp), device_id_type=MESH)
    kv_all[me] = kv_ref[...]
    log_all[me] = log_ref[...]
    pl.semaphore_wait(barrier, n - 1)

    def copies(k, slot):
        target = (pipe, lax.rem(me + k, n), tp)
        return (
            pltpu.make_async_remote_copy(
                kv_ref, kv_all.at[slot], kv_send.at[k], kv_recv.at[slot],
                device_id=target, device_id_type=MESH,
            ),
            pltpu.make_async_remote_copy(
                log_ref, log_all.at[slot], log_send.at[k], log_recv.at[slot],
                device_id=target, device_id_type=MESH,
            ),
        )

    for k in range(1, n):

        @pl.when(me + k < n)
        def _():
            for copy in copies(k, me):
                copy.start()
            kv_all[lax.rem(me + k, n)] = jnp.zeros_like(kv_ref)
            log_all[lax.rem(me + k, n)] = jnp.zeros_like(log_ref)

    for k in range(1, n):

        @pl.when(me + k >= n)
        def _():
            for copy in copies(k, lax.rem(me + k, n)):
                copy.wait_recv()

        @pl.when(me + k < n)
        def _():
            for copy in copies(k, me):
                copy.wait_send()


def share(kv, last, n):
    vmem = pl.BlockSpec(memory_space=pltpu.VMEM)
    logs = jnp.broadcast_to(last[None, :], (8, last.shape[0]))
    logs = jnp.pad(logs, ((0, 0), (0, -last.shape[0] % 128)))
    kv_all, log_all = pl.pallas_call(
        functools.partial(share_kernel, n),
        out_shape=(
            jax.ShapeDtypeStruct((n, *kv.shape), kv.dtype),
            jax.ShapeDtypeStruct((n, *logs.shape), logs.dtype),
        ),
        in_specs=[vmem] * 2,
        out_specs=(vmem, vmem),
        scratch_shapes=[pltpu.SemaphoreType.DMA((n,))] * 4,
        compiler_params=pltpu.CompilerParams(
            collective_id=0, has_side_effects=True, vmem_limit_bytes=32 * 2**20
        ),
        name="share",
    )(kv, logs)
    return kv_all.reshape(-1, kv.shape[1]), log_all[:, 0, : last.shape[0]]


def project_kernel(
    n, kept, outgoing, weights, resid, out,
    rows, staged, parts, first,
    row_recv, up_send, down_send, side_send, pipe_send, part_send, part_recv, first_send, first_recv,
):
    pipe, me, tp = (lax.axis_index(a) for a in ("pipe", "ctx", "tp"))
    line, half_n = n // 2, n // 2
    pos = me // 2
    side = me + 1 - 2 * lax.rem(me, 2)
    owner_tp, own_chunk = me // half_n, lax.rem(me, half_n)
    other = 1 - pipe
    width = weights.shape[1]
    depth = kept.shape[1]

    barrier = pltpu.get_barrier_semaphore()
    here = me * 2 + tp
    for k in range(1, 2 * n):
        there = lax.rem(here + k, 2 * n)
        pl.semaphore_signal(
            barrier, inc=1, device_id=(pipe, there // 2, lax.rem(there, 2)), device_id_type=MESH
        )
    pl.semaphore_signal(barrier, inc=1, device_id=(other, me, tp), device_id_type=MESH)
    rows[me, pipe] = kept[...]
    pl.semaphore_wait(barrier, 2 * n)

    def hop(c, h, sem, ctx):
        return pltpu.make_async_remote_copy(
            rows.at[c, h], rows.at[c, h], sem.at[c, h], row_recv.at[c, h],
            device_id=(pipe, ctx, tp), device_id_type=MESH,
        )

    def cross(h):
        return pltpu.make_async_remote_copy(
            outgoing, rows.at[me, h], pipe_send, row_recv.at[me, h],
            device_id=(other, me, tp), device_id_type=MESH,
        )

    up, down = jnp.minimum(me + 2, n - 1), jnp.maximum(me - 2, 0)
    can_up, can_down = pos + 1 < line, pos > 0

    def part_copy(c):
        return pltpu.make_async_remote_copy(
            staged.at[c], parts.at[own_chunk, tp], part_send.at[c], part_recv.at[own_chunk, tp],
            device_id=(pipe, c, owner_tp), device_id_type=MESH,
        )

    def is_mine(c):
        return (c == me) & (owner_tp == tp)

    cross(pipe).start()

    def forward(s, act):
        @pl.when(s == 0)
        def _():
            for turn in range(2):
                h = pipe if turn == 0 else other
                if turn == 1:
                    act(cross(other), None)

                @pl.when(can_up)
                def _():
                    act(None, hop(me, h, up_send, up))

                @pl.when(can_down)
                def _():
                    act(None, hop(me, h, down_send, down))

                act(None, hop(me, h, side_send, side))

        @pl.when((s > 0) & (s < line))
        def _():
            for turn in range(2):
                h = pipe if turn == 0 else other
                below, above = me - 2 * s, me + 2 * s

                @pl.when(below >= 0)
                def _():
                    act(hop(below, h, up_send, up), None)

                    @pl.when(can_up)
                    def _():
                        act(None, hop(below, h, up_send, up))

                    act(None, hop(below, h, side_send, side))

                @pl.when(above < n)
                def _():
                    act(hop(above, h, down_send, down), None)

                    @pl.when(can_down)
                    def _():
                        act(None, hop(above, h, down_send, down))

                    act(None, hop(above, h, side_send, side))

    def go(arrived, leaving):
        if arrived is not None:
            arrived.wait_recv()
        if leaving is not None:
            leaving.start()

    def drain(arrived, leaving):
        if leaving is not None:
            leaving.wait_send()

    def multiply(c):
        total = jnp.dot(rows[c, 0], weights[:depth], preferred_element_type=jnp.float32)
        total += jnp.dot(rows[c, 1], weights[depth:], preferred_element_type=jnp.float32)
        piece = total.astype(jnp.bfloat16)

        @pl.when(is_mine(c))
        def _():
            parts[own_chunk, tp] = piece

        @pl.when(jnp.logical_not(is_mine(c)))
        def _():
            staged[c] = piece
            part_copy(c).start()

    def turn(s, carry):
        forward(s, go)

        def block(k, carry):
            late = k // 2
            dist = s - late
            centre = me + late * (side - me)
            c = centre + (2 * lax.rem(k, 2) - 1) * 2 * dist
            ok = (dist >= 0) & (dist < line) & (c >= 0) & (c < n)
            ok = ok & ((dist > 0) | (lax.rem(k, 2) == 0))

            @pl.when(ok)
            def _():
                @pl.when(late == 1)
                def _():
                    for h in range(2):
                        hop(c, h, side_send, side).wait_recv()

                multiply(c)

            return carry

        return lax.fori_loop(0, 4, block, carry)

    lax.fori_loop(0, line + 1, turn, 0)

    def first_copy(q):
        return pltpu.make_async_remote_copy(
            first.at[q], first.at[q], first_send.at[q], first_recv.at[q],
            device_id=(other, me, tp), device_id_type=MESH,
        )

    for q in range(half_n):
        source = tp * half_n + q
        for t in range(2):

            @pl.when(jnp.logical_not((source == me) & (tp == t)))
            def _():
                pltpu.make_async_remote_copy(
                    parts.at[q, t], parts.at[q, t], part_send.at[0], part_recv.at[q, t],
                    device_id=(pipe, side, tp), device_id_type=MESH,
                ).wait_recv()

        total = parts[q, 0].astype(jnp.float32) + parts[q, 1].astype(jnp.float32)
        columns = slice(q * width, (q + 1) * width)

        @pl.when(pipe == 0)
        def _():
            done = (resid[:, columns].astype(jnp.float32) + total).astype(jnp.bfloat16)
            first[q] = done
            out[:, columns] = done
            first_copy(q).start()

        @pl.when(pipe == 1)
        def _():
            first_copy(q).wait_recv()
            out[:, columns] = (first[q].astype(jnp.float32) + total).astype(jnp.bfloat16)

    cross(pipe).wait_send()

    def finish(s, carry):
        forward(s, drain)
        return carry

    lax.fori_loop(0, line, finish, 0)

    def sent(c, carry):
        @pl.when(jnp.logical_not(is_mine(c)))
        def _():
            part_copy(c).wait_send()

        return carry

    lax.fori_loop(0, n, sent, 0)

    @pl.when(pipe == 0)
    def _():
        for q in range(half_n):
            first_copy(q).wait_send()


def project(kept, outgoing, weights, resid, n):
    vmem = pl.BlockSpec(memory_space=pltpu.VMEM)
    count, depth = kept.shape
    width = weights.shape[1]
    dma = pltpu.SemaphoreType.DMA
    return pl.pallas_call(
        functools.partial(project_kernel, n),
        out_shape=jax.ShapeDtypeStruct(resid.shape, jnp.bfloat16),
        in_specs=[vmem] * 4,
        out_specs=vmem,
        scratch_shapes=[
            pltpu.VMEM((n, 2, count, depth), jnp.bfloat16),
            pltpu.VMEM((n, count, width), jnp.bfloat16),
            pltpu.VMEM((n // 2, 2, count, width), jnp.bfloat16),
            pltpu.VMEM((n // 2, count, width), jnp.bfloat16),
            dma((n, 2)), dma((n, 2)), dma((n, 2)), dma((n, 2)), dma(()),
            dma((n,)), dma((n // 2, 2)), dma((n // 2,)), dma((n // 2,)),
        ],
        compiler_params=pltpu.CompilerParams(
            collective_id=1, has_side_effects=True, vmem_limit_bytes=56 * 2**20
        ),
        name="project",
    )(kept, outgoing, weights, resid)


def expand(per_head, width):
    return jnp.repeat(per_head, width, axis=1)


def mamba_local(x, b, c, step, rate, skip):
    rows, heads = step.shape
    log_decay = -step * rate[None, :]
    tri = jnp.arange(rows)[:, None] >= jnp.arange(rows)[None, :]
    running = jnp.dot(tri.astype(jnp.float32), log_decay, precision=exact_mode)
    cross = jnp.einsum("tn,sn->ts", c, b, preferred_element_type=jnp.float32)
    spread = running.T[:, :, None] - running.T[:, None, :]
    decay = jnp.exp(jnp.where(tri[None], spread, -jnp.inf))
    mixing = (cross[None] * decay * step.T[:, None, :]).astype(jnp.bfloat16)
    heads_x = x.reshape(rows, heads, MHEAD_DIM)
    within = jnp.einsum("hts,shp->thp", mixing, heads_x, preferred_element_type=jnp.float32)
    xf = x.astype(jnp.float32)
    within = within.reshape(rows, -1) + xf * jnp.repeat(skip, MHEAD_DIM)[None, :]
    tail = jnp.exp(running[-1:] - running) * step
    weighted = (xf * expand(tail, MHEAD_DIM)).astype(jnp.bfloat16)
    state = jnp.einsum("sp,sn->np", weighted, b, preferred_element_type=jnp.float32)
    return running, within, state


def entering_state(running, state, logs):
    peers, position = lax.axis_size("ctx"), lax.axis_index("ctx")
    span = jnp.arange(peers)
    own = jnp.exp(jnp.repeat(running[-1], MHEAD_DIM))[None, :]
    before = jnp.zeros_like(state)
    reach = 1
    while reach < peers:
        pairs = [(i, i + reach) for i in range(peers - reach)]
        sent = (state + own * before).astype(jnp.bfloat16)
        got = lax.ppermute(sent, "ctx", pairs).astype(jnp.float32)
        inside = (span < position) & (span > position - reach)
        through = jnp.sum(jnp.where(inside[:, None], logs, 0.0), axis=0)
        before = before + jnp.exp(jnp.repeat(through, MHEAD_DIM))[None, :] * got
        reach *= 2
    return before.astype(jnp.bfloat16)


def mamba_mixer(running, within, entering, gate, b, c, gains):
    carried = jnp.dot(c, entering, preferred_element_type=jnp.float32)
    y = within + carried * expand(jnp.exp(running), MHEAD_DIM)
    gated = y * jax.nn.silu(gate.astype(jnp.float32))
    per_group = gated.reshape(gated.shape[0], b.shape[1] // STATE, -1)
    meansq = jnp.mean(per_group * per_group, axis=-1, keepdims=True)
    scaled = (per_group * lax.rsqrt(meansq + norm_eps)).reshape(gated.shape)
    return (scaled * gains[None, :]).astype(jnp.bfloat16)


def attention(queries, both, ctx_rank):
    rows = queries.shape[0]
    k, v = both[:, :HEAD_DIM], both[:, HEAD_DIM:]
    heads = queries.shape[1] // HEAD_DIM
    q = queries.reshape(rows, heads, HEAD_DIM)
    scores = jnp.einsum("qjd,kd->jqk", q, k, preferred_element_type=jnp.float32)
    scores = scores * (1.0 / math.sqrt(HEAD_DIM))
    position = ctx_rank * rows + jnp.arange(rows)
    allowed = jnp.arange(k.shape[0])[None, :] <= position[:, None]
    scores = jnp.where(allowed[None], scores, -jnp.inf)
    weights = jnp.exp(scores - jnp.max(scores, axis=-1, keepdims=True))
    total = jnp.sum(weights, axis=-1)
    mixed = jnp.einsum("jqk,kd->qjd", weights.astype(jnp.bfloat16), v, preferred_element_type=jnp.float32)
    return (mixed / total.T[:, :, None]).reshape(rows, -1).astype(jnp.bfloat16)


def take_half(array, axis_dim, section):
    width = array.shape[axis_dim] // 2
    return lax.dynamic_slice_in_dim(array, section * width, width, axis_dim)


def per_device(
    resid_in,
    ssm_input,
    ssm_gate,
    ssm_in_b,
    ssm_out_c,
    step_size,
    decay_rate,
    skip_gain,
    norm_gain,
    queries,
    keys,
    values,
    out_weights,
):
    section = lax.axis_index("pipe")
    ctx_rank = lax.axis_index("ctx")
    peers = lax.axis_size("ctx")
    b = take_half(ssm_in_b, 1, section)
    c = take_half(ssm_out_c, 1, section)
    running, within, state = mamba_local(
        take_half(ssm_input, 1, section),
        b,
        c,
        take_half(step_size, 1, section),
        take_half(decay_rate, 0, section),
        take_half(skip_gain, 0, section),
    )
    kv = jnp.concatenate([take_half(keys, 1, section), take_half(values, 1, section)], axis=1)
    both, logs = share(kv, running[-1], peers)
    entering = entering_state(running, state, logs)
    mamba_part = mamba_mixer(
        running, within, entering, take_half(ssm_gate, 1, section), b, c,
        take_half(norm_gain, 0, section),
    )
    attn_part = attention(take_half(queries, 1, section), both, ctx_rank)
    outgoing = jnp.where(section == 0, attn_part, mamba_part)
    kept_half = jnp.where(section == 0, mamba_part, attn_part)
    return project(kept_half, outgoing, out_weights[0], resid_in, peers)[None]


def solution(mesh):
    return jax.shard_map(
        per_device,
        mesh=mesh,
        in_specs=(
            P("ctx", "tp"),
            P("ctx", "tp"),
            P("ctx", "tp"),
            P("ctx", "tp"),
            P("ctx", "tp"),
            P("ctx", "tp"),
            P("tp"),
            P("tp"),
            P("tp"),
            P("ctx", "tp"),
            P("ctx", "tp"),
            P("ctx", "tp"),
            P("pipe", "tp", "ctx"),
        ),
        out_specs=P("pipe", "ctx", "tp"),
        check_vma=False,
    )
```
